32 devices in a mesh: dp: 16 (over z, x, core), tensor: 2 (over y).
Axes of the slice: x: 2, y: 2, z: 4, core: 2. Of those that a mesh axis runs over, the one named last changes fastest.
Arguments:
- tokens: bfloat16 [16384, 1024], P(('dp', 'tensor')), may hold values from -6 to 6
- segments: int32 [16384], P(('dp', 'tensor')), may hold values from 0 to 4, as said below
- positions: int32 [16384], P(('dp', 'tensor')), may hold values from 0 to 2047, as said below
- query_weight: bfloat16 [1024, 2048], P('dp', 'tensor'), may hold values from -0.1875 to 0.1875
- key_matrix: bfloat16 [1024, 1024], P('dp', 'tensor'), may hold values from -0.1875 to 0.1875
- value_matrix: bfloat16 [1024, 1024], P('dp', 'tensor'), may hold values from -0.1875 to 0.1875
- out_weight: bfloat16 [2048, 1024], P('tensor', 'dp'), may hold values from -1 to 1
- gate_weight: bfloat16 [1024, 3072], P('dp', 'tensor'), may hold values from -0.1875 to 0.1875
- up_weight: bfloat16 [1024, 3072], P('dp', 'tensor'), may hold values from -0.1875 to 0.1875
- down_weight: bfloat16 [3072, 1024], P('tensor', 'dp'), may hold values from -0.109375 to 0.109375
- attn_gain: float32 [1024], replicated, may hold values from 0.1 to 1.9
- query_gain: float32 [128], replicated, may hold values from 0.1 to 1.9
- key_norm_gain: float32 [128], replicated, may hold values from 0.1 to 1.9
- ffn_gain: float32 [1024], replicated, may hold values from 0.1 to 1.9
- out_grad: bfloat16 [16384, 1024], P(('dp', 'tensor')), may hold values from -8 to 8
Outputs:
- layer_out: bfloat16 [16384, 1024], P(('dp', 'tensor'))
- tokens_grad: float32 [16384, 1024], P(('dp', 'tensor'))
- query_weight_grad: float32 [1024, 2048], P('dp', 'tensor')
- key_weight_grad: float32 [1024, 1024], P('dp', 'tensor')
- value_weight_grad: float32 [1024, 1024], P('dp', 'tensor')
- out_weight_grad: float32 [2048, 1024], P('tensor', 'dp')
- gate_weight_grad: float32 [1024, 3072], P('dp', 'tensor')
- up_weight_grad: float32 [1024, 3072], P('dp', 'tensor')
- down_weight_grad: float32 [3072, 1024], P('tensor', 'dp')
- attn_gain_grad: float32 [1024], replicated
- query_gain_grad: float32 [128], replicated
- key_gain_grad: float32 [128], replicated
- ffn_gain_grad: float32 [1024], replicated
The draws below stay inside these ranges and needn't reach their ends.
Inputs may be any that keep to these rules, and one draw needn't show every extreme that they name: `segments`: within each packed sequence of 1024 tokens the numbers never fall and take each of 0 to 4 on one or more tokens; document 2 begins within the sequence's first 512 tokens and ends within its last 512. `positions`: positions rise by one from token to token within a document; document 2 of every packed sequence ends at position 2047.
All inputs are finite; a program needn't handle non-finite values.
Results may differ from the reference program's by a relative error of at most 0.019.
Values may be sent and summed in bfloat16 or wider, within the bound.
A program may use at most 192 MiB of HBM per device.

```python
import jax
import jax.numpy as jnp
from jax import lax

MODEL_WIDTH = 1024
FF = 3072
QUERY_HEADS = 16
KEY_VALUE_HEADS = 8
HEAD_SIZE = 128
SEQ = 1024
PIECE = 512
TOKENS = 16384


def layout(key):
    groups = TOKENS // SEQ
    subkeys = jax.random.split(key, 5)
    long_start = jax.random.randint(subkeys[0], (groups, 1), 2, PIECE)
    first_cut = jax.random.randint(subkeys[1], (groups, 1), 1, long_start)
    finish = jax.random.randint(subkeys[2], (groups, 1), SEQ - PIECE + 1, SEQ - 1)
    last_cut = jax.random.randint(subkeys[3], (groups, 1), finish + 1, SEQ)
    places = jnp.arange(SEQ, dtype=jnp.int32)[None, :]
    doc_marks = (places >= first_cut).astype(jnp.int32) + (places >= long_start).astype(jnp.int32) + (places >= finish).astype(jnp.int32) + (places >= last_cut).astype(jnp.int32)
    begins = jnp.concatenate([jnp.zeros_like(long_start), first_cut, long_start, finish, last_cut], axis=1)
    offsets = jax.random.randint(subkeys[4], (groups, 5), 0, SEQ)
    column = jnp.arange(5, dtype=jnp.int32)[None, :]
    offsets = jnp.where(column == 2, 2 * SEQ - (finish - long_start), offsets)
    chosen = jnp.arange(5, dtype=jnp.int32)[None, None, :] == doc_marks[:, :, None]
    begin_at = jnp.sum(jnp.where(chosen, begins[:, None, :], 0), axis=-1)
    offset_at = jnp.sum(jnp.where(chosen, offsets[:, None, :], 0), axis=-1)
    return (doc_marks.reshape(-1), (places - begin_at + offset_at).reshape(-1))


def draw_segments(key, part):
    doc_marks, places = layout(key)
    return doc_marks


def draw_positions(key, part):
    doc_marks, places = layout(key)
    return places


def draw_out_grad(key, part):
    key = jax.random.fold_in(key, 7)
    row_rank = jnp.arange(TOKENS, dtype=jnp.float32)[:, None] / max(TOKENS - 1, 1)
    rising = 0.6 + 1.2 * row_rank
    base_draw = jnp.clip(jax.random.normal(key, (TOKENS, MODEL_WIDTH), jnp.float32), -4.0, 4.0)
    return (base_draw * rising).astype(jnp.bfloat16)


def block_levels(stream_key, extent, shards, low, high):
    factor_of, own = 1.0, jax.random.fold_in(stream_key, 6)
    for axis_at, blocks in shards:
        heights = jnp.exp(jax.random.uniform(jax.random.fold_in(own, axis_at), (blocks,), jnp.float32, low / len(shards), high / len(shards)))
        factor_of = factor_of * jnp.repeat(heights, extent[axis_at] // blocks).reshape([-1 if axis == axis_at else 1 for axis in range(len(extent))])
    return factor_of


def noise(rng, dims, spread, most, pieces=(), kind=jnp.bfloat16):
    factor_of = block_levels(rng, dims, pieces, -0.22, 0.18) if pieces else 1.0
    values = jax.random.normal(rng, dims, jnp.float32) * spread * factor_of
    return jnp.minimum(jnp.maximum(values, -most), most).astype(kind)


def setup_inputs(seed: int = 0) -> dict:
    key_of = jax.random.split(jax.random.key(seed), 16)
    tokens = noise(key_of[0], (TOKENS, MODEL_WIDTH), 1.0, 6.0, ((0, 32),))
    segments = draw_segments(jax.random.fold_in(key_of[15], 71), 0)
    positions = draw_positions(jax.random.fold_in(key_of[15], 71), 0)
    query_weight = noise(key_of[3], (MODEL_WIDTH, QUERY_HEADS * HEAD_SIZE), MODEL_WIDTH ** -0.5, 0.1875, ((0, 16), (1, 2)))
    key_matrix = noise(key_of[4], (MODEL_WIDTH, KEY_VALUE_HEADS * HEAD_SIZE), MODEL_WIDTH ** -0.5, 0.1875, ((0, 16), (1, 2)))
    value_matrix = noise(key_of[5], (MODEL_WIDTH, KEY_VALUE_HEADS * HEAD_SIZE), MODEL_WIDTH ** -0.5, 0.1875, ((0, 16), (1, 2)))
    out_weight = noise(key_of[6], (QUERY_HEADS * HEAD_SIZE, MODEL_WIDTH), (max(1, QUERY_HEADS * HEAD_SIZE * 16 // SEQ)) ** -0.5, 1.0, ((0, 2), (1, 16)))
    gate_weight = noise(key_of[7], (MODEL_WIDTH, FF), MODEL_WIDTH ** -0.5, 0.1875, ((0, 16), (1, 2)))
    up_weight = noise(key_of[8], (MODEL_WIDTH, FF), MODEL_WIDTH ** -0.5, 0.1875, ((0, 16), (1, 2)))
    down_weight = noise(key_of[9], (FF, MODEL_WIDTH), FF ** -0.5, 0.109375, ((0, 2), (1, 16)))
    attn_gain = jnp.clip(1.0 + 0.18 * jax.random.normal(key_of[10], (MODEL_WIDTH,), jnp.float32), 0.1, 1.9)
    query_gain = jnp.clip(1.0 + 0.18 * jax.random.normal(key_of[11], (HEAD_SIZE,), jnp.float32), 0.1, 1.9)
    key_norm_gain = jnp.clip(1.0 + 0.18 * jax.random.normal(key_of[12], (HEAD_SIZE,), jnp.float32), 0.1, 1.9)
    ffn_gain = jnp.clip(1.0 + 0.18 * jax.random.normal(key_of[13], (MODEL_WIDTH,), jnp.float32), 0.1, 1.9)
    out_grad = draw_out_grad(jax.random.fold_in(key_of[15], 71), 0)
    return dict(tokens=tokens, segments=segments, positions=positions, query_weight=query_weight, key_matrix=key_matrix, value_matrix=value_matrix, out_weight=out_weight, gate_weight=gate_weight, up_weight=up_weight, down_weight=down_weight, attn_gain=attn_gain, query_gain=query_gain, key_norm_gain=key_norm_gain, ffn_gain=ffn_gain, out_grad=out_grad)


EPSILON = 1e-06
ROPE_BASE = 1000000.0
NEGATIVE = -1e+30
PRECISE = lax.Precision.HIGHEST

@jax.custom_vjp
def lowered_copy(v):
    return lax.optimization_barrier(v.astype(jnp.bfloat16)).astype(jnp.float32)

@jax.custom_vjp
def low_back(v):
    return v

def low_keep(v):
    return (lowered_copy(v), None)

def low_pass(kept, grad):
    return (grad,)

def back_keep(v):
    return (v, None)

def back_low(kept, grad):
    return (lowered_copy(grad),)
lowered_copy.defvjp(low_keep, low_pass)
low_back.defvjp(back_keep, back_low)

def root_mean_norm(values, gain_row):
    factor = lax.rsqrt(lax.optimization_barrier(jnp.mean(values * values, axis=-1, keepdims=True)) + EPSILON)
    return values * factor * gain_row

def rotary_apply(values, cosine_table, sine_values):
    middle = values.shape[-1] // 2
    turned = jnp.concatenate([-values[..., middle:], values[..., :middle]], axis=-1)
    return values * cosine_table + turned * sine_values

def tables(places, head_dim):
    middle = head_dim // 2
    powers = jnp.arange(middle, dtype=jnp.float32) * (2.0 / head_dim)
    inverse = jnp.power(ROPE_BASE, -powers)
    angles = places.astype(jnp.float32)[:, None] * inverse[None, :]
    angles = jnp.concatenate([angles, angles], axis=-1)
    return (jnp.cos(angles)[:, None, :], jnp.sin(angles)[:, None, :])

def attend(query_rows, key_matrix_rows, value_matrix_rows, seg_marks):
    row_length = query_rows.shape[0]
    tile_rows = min(512, row_length)
    heads_per_group = QUERY_HEADS // KEY_VALUE_HEADS
    keys_wide = jnp.repeat(key_matrix_rows, heads_per_group, axis=1)
    values_wide = jnp.repeat(value_matrix_rows, heads_per_group, axis=1)
    key_order = jnp.arange(row_length, dtype=jnp.int32)
    score_scale = HEAD_SIZE ** (-0.5)

    def one_block(start_row):
        q_block = lax.dynamic_slice_in_dim(query_rows, start_row, tile_rows, 0)
        marks_block = lax.dynamic_slice_in_dim(seg_marks, start_row, tile_rows, 0)
        places = start_row + jnp.arange(tile_rows, dtype=jnp.int32)
        scores = low_back(jnp.einsum('qhd,khd->hqk', q_block, keys_wide, precision=PRECISE) * score_scale)
        allowed = (marks_block[:, None] == seg_marks[None, :]) & (places[:, None] >= key_order[None, :])
        scores = jnp.where(allowed[None], scores, NEGATIVE)
        weights = lowered_copy(jax.nn.softmax(scores, axis=-1))
        return jnp.einsum('hqk,khd->qhd', weights, values_wide, precision=PRECISE)
    starts = jnp.arange(row_length // tile_rows, dtype=jnp.int32) * tile_rows
    return lax.map(jax.checkpoint(one_block), starts).reshape(row_length, QUERY_HEADS, HEAD_SIZE)

def group_layer(params, sequence):
    query_weight, key_matrix, value_matrix, out_weight, gate_weight, up_weight, down_weight, attn_gain, query_gain, key_norm_gain, ffn_gain = params
    tokens, seg_marks, places = sequence
    row_length = tokens.shape[0]
    normed_first = lowered_copy(root_mean_norm(tokens, attn_gain))
    query_raw = low_back(jnp.dot(normed_first, query_weight, precision=PRECISE))
    key_unrotated = low_back(jnp.dot(normed_first, key_matrix, precision=PRECISE))
    value_unprojected = lowered_copy(low_back(jnp.dot(normed_first, value_matrix, precision=PRECISE)))
    cosine_table, sine_values = tables(places, HEAD_SIZE)
    query_rows = lowered_copy(rotary_apply(root_mean_norm(query_raw.reshape(row_length, QUERY_HEADS, HEAD_SIZE), query_gain), cosine_table, sine_values))
    key_matrix_rows = lowered_copy(rotary_apply(root_mean_norm(key_unrotated.reshape(row_length, KEY_VALUE_HEADS, HEAD_SIZE), key_norm_gain), cosine_table, sine_values))
    value_matrix_rows = value_unprojected.reshape(row_length, KEY_VALUE_HEADS, HEAD_SIZE)
    mixed_rows = low_back(lowered_copy(attend(query_rows, key_matrix_rows, value_matrix_rows, seg_marks).reshape(row_length, QUERY_HEADS * HEAD_SIZE)))
    hidden = tokens + low_back(jnp.dot(mixed_rows, out_weight, precision=PRECISE))
    second = lowered_copy(root_mean_norm(hidden, ffn_gain))
    gate_rows = low_back(jnp.dot(second, gate_weight, precision=PRECISE))
    up_rows = low_back(jnp.dot(second, up_weight, precision=PRECISE))
    activated = lowered_copy(jax.nn.silu(gate_rows) * up_rows)
    return hidden + low_back(jnp.dot(activated, down_weight, precision=PRECISE))

def forward(params, tokens, segments, positions):
    feature_dim = tokens.shape[1]
    sequences = (tokens.reshape(-1, SEQ, feature_dim), segments.reshape(-1, SEQ), positions.reshape(-1, SEQ))

    def scan_step(carried, sequence):
        return (carried, jax.checkpoint(group_layer)(params, sequence))
    unused, outputs = lax.scan(scan_step, None, sequences)
    return outputs.reshape(-1, feature_dim)

def reference(tokens, segments, positions, query_weight, key_matrix, value_matrix, out_weight, gate_weight, up_weight, down_weight, attn_gain, query_gain, key_norm_gain, ffn_gain, out_grad):
    params = tuple((matrix.astype(jnp.float32) for matrix in (query_weight, key_matrix, value_matrix, out_weight, gate_weight, up_weight, down_weight, attn_gain, query_gain, key_norm_gain, ffn_gain)))
    inputs = tokens.astype(jnp.float32)

    def apply_layer(layer_params, layer_inputs):
        return forward(layer_params, layer_inputs, segments, positions)
    result, pull_back = jax.vjp(apply_layer, params, inputs)
    param_grads, tokens_grad = pull_back(out_grad.astype(jnp.float32))
    return (result.astype(jnp.bfloat16), tokens_grad, param_grads[0], param_grads[1], param_grads[2], param_grads[3], param_grads[4], param_grads[5], param_grads[6], param_grads[7], param_grads[8], param_grads[9], param_grads[10])
```

```python
import jax
import jax.numpy as jnp
from jax import lax
from jax.sharding import PartitionSpec as P

EPSILON = 1e-06
ROPE_BASE = 1000000.0
NEGATIVE = -1e30


def root_mean_norm(values, gain_row):
    factor = lax.rsqrt(jnp.mean(values * values, axis=-1, keepdims=True) + EPSILON)
    return values * factor * gain_row


def rotary_apply(values, cosine_table, sine_values):
    middle = values.shape[-1] // 2
    turned = jnp.concatenate([-values[..., middle:], values[..., :middle]], axis=-1)
    return values * cosine_table + turned * sine_values


def tables(places, head_dim):
    middle = head_dim // 2
    powers = jnp.arange(middle, dtype=jnp.float32) * (2.0 / head_dim)
    inverse = jnp.power(ROPE_BASE, -powers)
    angles = places.astype(jnp.float32)[:, None] * inverse[None, :]
    angles = jnp.concatenate([angles, angles], axis=-1)
    return (jnp.cos(angles)[:, None, :], jnp.sin(angles)[:, None, :])


def silu_product(gate_rows, up_rows):
    return jax.nn.silu(gate_rows) * up_rows


def matmul(left_side, right_side):
    return jnp.dot(left_side, right_side, preferred_element_type=jnp.float32)


def left_contract(left_side, right_side):
    return lax.dot_general(
        left_side, right_side, (((0,), (0,)), ((), ())), preferred_element_type=jnp.float32
    )


def right_contract(left_side, right_side):
    return lax.dot_general(
        left_side, right_side, (((1,), (1,)), ((), ())), preferred_element_type=jnp.float32
    )


def tile_mask(q_marks, k_marks, q_start, k_start):
    q_places = q_start + jnp.arange(q_marks.shape[0])
    k_places = k_start + jnp.arange(k_marks.shape[0])
    return (q_marks[:, None] == k_marks[None, :]) & (q_places[:, None] >= k_places[None, :])


def tile_scores(q_block, k_block, allowed, score_scale):
    scores = (
        jnp.einsum("qgsd,kgd->gsqk", q_block, k_block, preferred_element_type=jnp.float32)
        * score_scale
    )
    return jnp.where(allowed, scores, NEGATIVE)


def attend_forward(
    query_rows, key_matrix_rows, value_matrix_rows, row_marks, tile_rows, score_scale
):
    seq_rows, groups, heads_per_group, head_dim = query_rows.shape
    tile_count = seq_rows // tile_rows
    mixed_parts, full_parts, total_parts = ([], [], [])
    for q_index in range(tile_count):
        q_start = q_index * tile_rows
        q_block = query_rows[q_start : q_start + tile_rows]
        q_marks = row_marks[q_start : q_start + tile_rows]
        running = jnp.full((groups, heads_per_group, tile_rows), NEGATIVE, jnp.float32)
        totals = jnp.zeros((groups, heads_per_group, tile_rows), jnp.float32)
        for k_index in range(q_index + 1):
            k_start = k_index * tile_rows
            allowed = tile_mask(q_marks, row_marks[k_start : k_start + tile_rows], q_start, k_start)
            scores = tile_scores(
                q_block, key_matrix_rows[k_start : k_start + tile_rows], allowed, score_scale
            )
            newest = jnp.maximum(running, jnp.max(scores, axis=-1))
            fresh = jnp.where(allowed, jnp.exp(scores - newest[..., None]), 0.0)
            totals = totals * jnp.exp(running - newest) + jnp.sum(fresh, axis=-1)
            running = newest
        log_totals = running + jnp.log(totals)
        upper_sum = jnp.zeros((tile_rows, groups, heads_per_group, head_dim), jnp.float32)
        lower_sum = jnp.zeros((tile_rows, groups, heads_per_group, head_dim), jnp.float32)
        for k_index in range(q_index + 1):
            k_start = k_index * tile_rows
            allowed = tile_mask(q_marks, row_marks[k_start : k_start + tile_rows], q_start, k_start)
            scores = tile_scores(
                q_block, key_matrix_rows[k_start : k_start + tile_rows], allowed, score_scale
            )
            probs_tile = jnp.where(allowed, jnp.exp(scores - log_totals[..., None]), 0.0)
            high_part = probs_tile.astype(jnp.bfloat16)
            low_part = (probs_tile - high_part.astype(jnp.float32)).astype(jnp.bfloat16)
            v_block = value_matrix_rows[k_start : k_start + tile_rows]
            upper_sum = upper_sum + jnp.einsum(
                "gsqk,kgd->qgsd", high_part, v_block, preferred_element_type=jnp.float32
            )
            lower_sum = lower_sum + jnp.einsum(
                "gsqk,kgd->qgsd", low_part, v_block, preferred_element_type=jnp.float32
            )
        mixed_parts.append(upper_sum.astype(jnp.bfloat16))
        full_parts.append(upper_sum + lower_sum)
        total_parts.append(log_totals)
    return (
        jnp.concatenate(mixed_parts, 0),
        jnp.concatenate(full_parts, 0),
        jnp.concatenate(total_parts, -1),
    )


def attend_backward(
    query_rows,
    key_matrix_rows,
    value_matrix_rows,
    row_marks,
    log_totals,
    full_mixed,
    grad_mixed,
    tile_rows,
    score_scale,
):
    seq_rows, groups, heads_per_group, head_dim = query_rows.shape
    tile_count = seq_rows // tile_rows
    delta_rows = jnp.einsum("qgsd,qgsd->gsq", grad_mixed.astype(jnp.float32), full_mixed)
    key_grads = [
        jnp.zeros((tile_rows, groups, head_dim), jnp.float32) for k_index in range(tile_count)
    ]
    value_grads = [
        jnp.zeros((tile_rows, groups, head_dim), jnp.float32) for k_index in range(tile_count)
    ]
    query_grads = []
    for q_index in range(tile_count):
        q_start = q_index * tile_rows
        q_block = query_rows[q_start : q_start + tile_rows]
        grad_block = grad_mixed[q_start : q_start + tile_rows]
        q_marks = row_marks[q_start : q_start + tile_rows]
        part_delta = delta_rows[..., q_start : q_start + tile_rows]
        part_totals = log_totals[..., q_start : q_start + tile_rows]
        query_accum = jnp.zeros((tile_rows, groups, heads_per_group, head_dim), jnp.float32)
        for k_index in range(q_index + 1):
            k_start = k_index * tile_rows
            k_block = key_matrix_rows[k_start : k_start + tile_rows]
            v_block = value_matrix_rows[k_start : k_start + tile_rows]
            allowed = tile_mask(q_marks, row_marks[k_start : k_start + tile_rows], q_start, k_start)
            scores = tile_scores(q_block, k_block, allowed, score_scale)
            probs_tile = jnp.where(allowed, jnp.exp(scores - part_totals[..., None]), 0.0)
            grad_probs = jnp.einsum(
                "qgsd,kgd->gsqk", grad_block, v_block, preferred_element_type=jnp.float32
            )
            grad_scores = (probs_tile * (grad_probs - part_delta[..., None])).astype(jnp.bfloat16)
            query_accum = (
                query_accum
                + jnp.einsum(
                    "gsqk,kgd->qgsd", grad_scores, k_block, preferred_element_type=jnp.float32
                )
                * score_scale
            )
            key_grads[k_index] = (
                key_grads[k_index]
                + jnp.einsum(
                    "gsqk,qgsd->kgd", grad_scores, q_block, preferred_element_type=jnp.float32
                )
                * score_scale
            )
            value_grads[k_index] = value_grads[k_index] + jnp.einsum(
                "gsqk,qgsd->kgd",
                probs_tile.astype(jnp.bfloat16),
                grad_block,
                preferred_element_type=jnp.float32,
            )
        query_grads.append(query_accum)
    return (
        jnp.concatenate(query_grads, 0),
        jnp.concatenate(key_grads, 0),
        jnp.concatenate(value_grads, 0),
    )


def swap_rows(values):
    return lax.ppermute(values, "tensor", [(0, 1), (1, 0)])


def row_blocks(own):
    if lax.axis_size("tensor") == 2:
        return [own, swap_rows(own)]
    return [lax.all_gather(own, "tensor", axis=0, tiled=True)]


def in_order(blocks):
    if len(blocks) == 1:
        return blocks[0]
    own, other = blocks
    first = lax.axis_index("tensor") == 0
    return jnp.concatenate([jnp.where(first, own, other), jnp.where(first, other, own)], 0)


def split_order(whole):
    if lax.axis_size("tensor") != 2:
        return [whole]
    half = whole.shape[0] // 2
    at = lax.axis_index("tensor") * half
    return [
        lax.dynamic_slice_in_dim(whole, at, half, 0),
        lax.dynamic_slice_in_dim(whole, half - at, half, 0),
    ]


def sum_rows(blocks, product):
    if len(blocks) == 1:
        return lax.psum_scatter(
            product(blocks[0]).astype(jnp.bfloat16), "tensor", scatter_dimension=0, tiled=True
        ).astype(jnp.float32)
    other = swap_rows(product(blocks[1]).astype(jnp.bfloat16))
    return product(blocks[0]) + other.astype(jnp.float32)


def gather_weights(parts):
    return lax.all_gather(jnp.concatenate(parts, 1), "dp", axis=0, tiled=True)


def side_by_side(parts):
    return jnp.concatenate([part.astype(jnp.bfloat16) for part in parts], 1)


def scatter_grads(whole):
    summed = lax.psum_scatter(whole, "dp", scatter_dimension=0, tiled=True)
    return summed.astype(jnp.float32)


def sum_everywhere(values):
    for axis in ("dp", "tensor"):
        count = lax.axis_size(axis)
        step = 1
        while step < count:
            values = values + lax.ppermute(
                values, axis, [(index, index ^ step) for index in range(count)]
            )
            step *= 2
    return values


def per_device(
    tokens,
    segments,
    positions,
    query_weight,
    key_matrix,
    value_matrix,
    out_weight,
    gate_weight,
    up_weight,
    down_weight,
    attn_gain,
    query_gain,
    key_norm_gain,
    ffn_gain,
    out_grad,
):
    tok_rows, width = tokens.shape
    head_dim = query_gain.shape[0]
    seq_rows = tok_rows * lax.axis_size("tensor")
    q_cols, kv_cols = query_weight.shape[1], key_matrix.shape[1]
    units = gate_weight.shape[1]
    q_heads = q_cols // head_dim
    kv_heads = kv_cols // head_dim
    heads_per_group = q_heads // kv_heads
    tile_rows = min(512, seq_rows)
    score_scale = head_dim ** (-0.5)
    inputs = tokens.astype(jnp.float32)
    marks_places = jnp.stack([segments, positions], 1)
    whole_marks = in_order(row_blocks(marks_places))
    row_marks, row_places = whole_marks[:, 0], whole_marks[:, 1]
    whole_tokens = in_order(row_blocks(tokens))
    full_attn = gather_weights([query_weight, key_matrix, value_matrix, out_weight.T])
    full_qkv = full_attn[:, : q_cols + 2 * kv_cols]
    full_out = full_attn[:, q_cols + 2 * kv_cols :]
    full_ffn = gather_weights([gate_weight, up_weight, down_weight.T])
    full_query = full_qkv[:, :q_cols]
    full_key = full_qkv[:, q_cols : q_cols + kv_cols]
    full_value = full_qkv[:, q_cols + kv_cols :]
    full_gate = full_ffn[:, :units]
    full_up = full_ffn[:, units : 2 * units]
    full_down = full_ffn[:, 2 * units :]
    unused_first, first_pull = jax.vjp(root_mean_norm, inputs, attn_gain)
    first_rows = root_mean_norm(whole_tokens.astype(jnp.float32), attn_gain).astype(jnp.bfloat16)
    cosine_table, sine_values = tables(row_places, head_dim)

    def head_prep(raw_cols, gain_row):
        heads = raw_cols.reshape(seq_rows, raw_cols.shape[1] // head_dim, head_dim)
        return rotary_apply(root_mean_norm(heads, gain_row), cosine_table, sine_values)

    query_raw = matmul(first_rows, full_query)
    key_unrotated = matmul(first_rows, full_key)
    value_matrix_rows = (
        matmul(first_rows, full_value).astype(jnp.bfloat16).reshape(seq_rows, kv_heads, head_dim)
    )
    query_rot, query_pull = jax.vjp(head_prep, query_raw, query_gain)
    key_rot, key_pull = jax.vjp(head_prep, key_unrotated, key_norm_gain)
    query_rows = query_rot.astype(jnp.bfloat16).reshape(
        seq_rows, kv_heads, heads_per_group, head_dim
    )
    key_matrix_rows = key_rot.astype(jnp.bfloat16)
    mixed_heads, full_mixed, log_totals = attend_forward(
        query_rows, key_matrix_rows, value_matrix_rows, row_marks, tile_rows, score_scale
    )
    mixed_rows = mixed_heads.reshape(seq_rows, q_heads * head_dim)
    hidden = inputs + sum_rows(
        split_order(mixed_rows), lambda rows: right_contract(rows, full_out)
    )
    second_own = root_mean_norm(hidden, ffn_gain)
    second_blocks = row_blocks(second_own.astype(jnp.bfloat16))
    grad_blocks = row_blocks(out_grad)
    unused_second, second_pull = jax.vjp(root_mean_norm, hidden, ffn_gain)
    act_blocks, gate_lows, up_lows = [], [], []
    for second_rows, grad_rows in zip(second_blocks, grad_blocks):
        gate_rows = matmul(second_rows, full_gate)
        up_rows = matmul(second_rows, full_up)
        activated, act_pull = jax.vjp(silu_product, gate_rows, up_rows)
        act_blocks.append(activated.astype(jnp.bfloat16))
        grad_gate, grad_up = act_pull(matmul(grad_rows, full_down))
        gate_lows.append(grad_gate.astype(jnp.bfloat16))
        up_lows.append(grad_up.astype(jnp.bfloat16))
    grad_second = sum_rows(
        list(zip(gate_lows, up_lows)),
        lambda lows: right_contract(lows[0], full_gate) + right_contract(lows[1], full_up),
    )
    layer_out = (
        hidden + sum_rows(act_blocks, lambda rows: right_contract(rows, full_down))
    ).astype(jnp.bfloat16)
    second_rows = jnp.concatenate(second_blocks, 0)
    ffn_parts = side_by_side(
        [
            left_contract(second_rows, jnp.concatenate(gate_lows, 0)),
            left_contract(second_rows, jnp.concatenate(up_lows, 0)),
            left_contract(jnp.concatenate(grad_blocks, 0), jnp.concatenate(act_blocks, 0)),
        ]
    )
    ffn_grads = scatter_grads(ffn_parts)
    grad_second = lax.optimization_barrier((grad_second, ffn_parts))[0]
    grad_norm, ffn_gain_part = second_pull(grad_second)
    grad_hidden = out_grad.astype(jnp.float32) + grad_norm
    attn_rows = in_order(row_blocks(grad_hidden.astype(jnp.bfloat16)))
    grad_mixed = matmul(attn_rows, full_out).astype(jnp.bfloat16)
    out_weight_part = left_contract(attn_rows, mixed_rows)
    grad_query, grad_key, grad_value = attend_backward(
        query_rows,
        key_matrix_rows,
        value_matrix_rows,
        row_marks,
        log_totals,
        full_mixed,
        grad_mixed.reshape(seq_rows, kv_heads, heads_per_group, head_dim),
        tile_rows,
        score_scale,
    )
    query_back, query_gain_part = query_pull(grad_query.reshape(seq_rows, q_heads, head_dim))
    key_back, key_gain_part = key_pull(grad_key)
    qkv_low = jnp.concatenate(
        [
            query_back.astype(jnp.bfloat16),
            key_back.astype(jnp.bfloat16),
            grad_value.reshape(seq_rows, kv_cols).astype(jnp.bfloat16),
        ],
        1,
    )
    grad_first = sum_rows(
        split_order(qkv_low), lambda rows: right_contract(rows, full_qkv)
    )
    attn_grads = scatter_grads(
        side_by_side([left_contract(first_rows, qkv_low), out_weight_part])
    )
    grad_inputs, attn_gain_part = first_pull(grad_first)
    tokens_grad = grad_hidden + grad_inputs
    gain_grads = sum_everywhere(
        jnp.concatenate([attn_gain_part, ffn_gain_part, query_gain_part, key_gain_part])
    )
    return (
        layer_out,
        tokens_grad,
        attn_grads[:, :q_cols],
        attn_grads[:, q_cols : q_cols + kv_cols],
        attn_grads[:, q_cols + kv_cols : q_cols + 2 * kv_cols],
        attn_grads[:, q_cols + 2 * kv_cols :].T,
        ffn_grads[:, :units],
        ffn_grads[:, units : 2 * units],
        ffn_grads[:, 2 * units :].T,
        gain_grads[:width],
        gain_grads[2 * width : 2 * width + head_dim],
        gain_grads[2 * width + head_dim :],
        gain_grads[width : 2 * width],
    )


def solution(mesh):
    return jax.shard_map(
        per_device,
        mesh=mesh,
        in_specs=(
            P(("dp", "tensor"), None),
            P(("dp", "tensor")),
            P(("dp", "tensor")),
            P("dp", "tensor"),
            P("dp", "tensor"),
            P("dp", "tensor"),
            P("tensor", "dp"),
            P("dp", "tensor"),
            P("dp", "tensor"),
            P("tensor", "dp"),
            P(),
            P(),
            P(),
            P(),
            P(("dp", "tensor"), None),
        ),
        out_specs=(
            P(("dp", "tensor"), None),
            P(("dp", "tensor"), None),
            P("dp", "tensor"),
            P("dp", "tensor"),
            P("dp", "tensor"),
            P("tensor", "dp"),
            P("dp", "tensor"),
            P("dp", "tensor"),
            P("tensor", "dp"),
            P(),
            P(),
            P(),
            P(),
        ),
        check_vma=False,
    )
```
